256 devices in a mesh: replica: 8 (over y, x_hi), fsdp: 32 (over x_lo, z, core).
Axes of the slice: x: 4 (x_hi: 2, x_lo: 2; x = x_hi * 2 + x_lo), y: 4, z: 8, core: 2. Of those that a mesh axis runs over, the one named last changes fastest.
Arguments:
- token_ids: int32 [32768], P(('replica', 'fsdp')), may hold values from 0 to 128000, as said below
- inputs: bfloat16 [32768, 8192], P(('replica', 'fsdp')), may hold values from -24 to 24
- key_cotangent: bfloat16 [32768, 768], P(('replica', 'fsdp')), may hold values from -6 to 6
- key_weight: float32 [8, 8192, 768], P('replica', 'fsdp'), may hold values from -0.0625 to 0.0625
- adam_m: float32 [8, 8192, 768], P('replica', 'fsdp'), may hold values from -0.25 to 0.25
- adam_v: float32 [8, 8192, 768], P('replica', 'fsdp'), may hold values from 2.4414063e-05 to 0.0024414062
- frag_local: float32 [8, 3, 8192, 512], P('replica', None, 'fsdp'), may hold values from -0.0625 to 0.0625
- frag_global: float32 [8, 8192, 512], P('replica', 'fsdp'), may hold values from -0.0625 to 0.0625
- outer_mom: float32 [8, 8192, 512], P('replica', 'fsdp'), may hold values from -0.15625 to 0.15625
- owner: int32 [32], P('fsdp'), may hold values from 0 to 7
- fragment: int32 [8], P('replica'), may hold values from 0 to 2
Outputs:
- input_cotangent: bfloat16 [32768, 8192], P(('replica', 'fsdp'))
- new_weight: float32 [8, 8192, 768], P('replica', 'fsdp')
- new_m: float32 [8, 8192, 768], P('replica', 'fsdp')
- new_v: float32 [8, 8192, 768], P('replica', 'fsdp')
- synced: float32 [8, 8192, 512], P('replica', 'fsdp')
- new_outer_mom: float32 [8, 8192, 512], P('replica', 'fsdp')
The draws below stay inside these ranges and needn't reach their ends.
Inputs may be any that keep to these rules, and one draw needn't show every extreme that they name: `token_ids`: token 0 of every replica's sequence of 4096 tokens is 128000, the id that begins a document; the same id begins every later document.
All inputs are finite; a program needn't handle non-finite values.
Results may differ from the reference program's by a relative error of at most 0.0095.
Values may be sent and summed in bfloat16 or wider, within the bound.
No kernel may reach another device: no remote copies, remote signals or barrier semaphores. Data moves between devices by JAX's collectives and lax.ppermute only.
A program may use at most 128 MiB of HBM per device.

```python
import math
import jax
import jax.numpy as jnp
from jax import lax

D = 8192
HEAD = 128
FW = 512
NFRAG = 3
TOK_DEV = 128
KVW = 768
SEQ = 4096
REPLICAS = 8
TOKENS = 32768
N_FSDP = 32


def draw_token_ids(key, part):
    word_key = jax.random.fold_in(key, 11)
    start_key = jax.random.fold_in(key, 12)
    word_ids = jax.random.randint(word_key, (TOKENS,), 0, 128000, dtype=jnp.int32)
    start_marks = jax.random.randint(start_key, (TOKENS,), 0, 4 * TOK_DEV, dtype=jnp.int32)
    token_index = jnp.arange(TOKENS, dtype=jnp.int32)
    is_first = token_index % SEQ == 0
    return jnp.where(is_first | (start_marks == 0), 128000, word_ids).astype(jnp.int32)


def plant(values, own_key, least, high):
    index_at = [jax.random.randint(jax.random.fold_in(own_key, axis), (), 0, length) for axis, length in enumerate(values.shape)]
    longest = values.shape.index(max(values.shape))
    beside = index_at[:longest] + [(index_at[longest] + 1) % values.shape[longest]] + index_at[longest + 1:]
    return values.at[tuple(index_at)].set(least).at[tuple(beside)].set(high)


def strengthened(drawn, own_key, source, target, parts, factor):
    owner, partner = [(jnp.arange(drawn.shape[dim]) // (drawn.shape[dim] // parts)).reshape([-1 if axis == dim else 1 for axis in range(drawn.ndim)]) for dim in (source, target)]
    chosen = jax.random.permutation(own_key, parts)[partner]
    strong = (owner == chosen) | (owner == (partner + parts // 2) % parts)
    return jnp.where(strong, factor * drawn, drawn)


def block_levels(own_key, extent, cuts, low, largest):
    factor_of, own = 1.0, jax.random.fold_in(own_key, 6)
    for axis_at, shards_of in cuts:
        draws = jnp.exp(jax.random.uniform(jax.random.fold_in(own, axis_at), (shards_of,), jnp.float32, low / len(cuts), largest / len(cuts)))
        factor_of = factor_of * jnp.repeat(draws, extent[axis_at] // shards_of).reshape([-1 if axis == axis_at else 1 for axis in range(len(extent))])
    return factor_of


def bell_draw(key, dims, spread, limit, shards=(), kind=jnp.bfloat16):
    array = jax.random.normal(key, dims, jnp.float32) * spread
    if len(shards) > 0:
        array = block_levels(key, dims, shards, -0.22, 0.18) * array
    return jnp.clip(array, min=-limit, max=limit).astype(kind)


def noise_with(rng, dims, scale, reach, pieces, heavy, kind=jnp.bfloat16):
    drawn = scale * jax.random.normal(rng, dims, jnp.float32)
    if pieces:
        drawn = drawn * block_levels(rng, dims, pieces, -0.22, 0.18)
    return jnp.clip(strengthened(drawn, jax.random.fold_in(rng, 3), *heavy), -reach, reach).astype(kind)


def setup_inputs(seed: int = 0) -> dict:
    splits = jax.random.split(jax.random.key(seed), 12)
    token_ids = draw_token_ids(jax.random.fold_in(splits[11], 71), 0)
    inputs = noise_with(splits[1], (TOKENS, D), 1.0, 24.0, ((0, 256),), (0, 1, 256, 6.0))
    key_cotangent = bell_draw(splits[2], (TOKENS, KVW), 1.0, 6.0, ((0, 256),))
    key_weight = bell_draw(splits[3], (REPLICAS, D, KVW), D ** -0.5, 0.0625, ((0, 8), (1, 32)), jnp.float32)
    adam_m = bell_draw(splits[4], (REPLICAS, D, KVW), (SEQ ** -0.5), 0.25, ((0, 8), (1, 32)), jnp.float32)
    adam_v = jnp.clip(jnp.exp(math.log(0.0024414062) - 4.6051702 * jax.random.uniform(splits[5], (REPLICAS, D, KVW), jnp.float32) ** block_levels(splits[5], (REPLICAS, D, KVW), ((0, 8), (1, 32)), -0.2, 0.2)), 2.441406286379788e-05, 0.0024414062)
    frag_local = bell_draw(splits[6], (REPLICAS, NFRAG, D, FW), D ** -0.5, 0.0625, ((0, 8), (2, 32)), jnp.float32)
    frag_global = bell_draw(splits[7], (REPLICAS, D, FW), D ** -0.5, 0.0625, ((0, 8), (1, 32)), jnp.float32)
    outer_mom = bell_draw(splits[8], (REPLICAS, D, FW), (D ** -0.5), 0.15625, ((0, 8), (1, 32)), jnp.float32)
    owner = plant(jax.random.randint(splits[9], (N_FSDP,), 0, REPLICAS), jax.random.fold_in(splits[9], 1), 0, REPLICAS - 1).astype(jnp.int32)
    fragment = plant(jax.random.randint(splits[10], (REPLICAS,), 0, NFRAG), jax.random.fold_in(splits[10], 1), 0, NFRAG - 1).astype(jnp.int32)
    return {"token_ids": token_ids, "inputs": inputs, "key_cotangent": key_cotangent, "key_weight": key_weight, "adam_m": adam_m, "adam_v": adam_v, "frag_local": frag_local, "frag_global": frag_global, "outer_mom": outer_mom, "owner": owner, "fragment": fragment}


begin_token = 128000
rope_base = 500000.0
beta_one = 0.9
beta_two = 0.95
adam_lr = 0.001
adam_eps = 1e-08
adam_step = 10.0
weight_decay = 0.1
outer_lr = 0.7
outer_momentum = 0.9

def unrotate(cotangent, positions):
    row_count = cotangent.shape[0]
    head_count = cotangent.shape[1] // HEAD
    half_head = HEAD // 2
    frequency = jnp.float32(rope_base) ** (-(jnp.arange(half_head, dtype=jnp.float32) * (2.0 / HEAD)))
    angles = positions.astype(jnp.float32)[:, None] * frequency[None, :]
    cosine = jnp.cos(angles)[:, None, :]
    sine_part = jnp.sin(angles)[:, None, :]
    per_head = cotangent.astype(jnp.float32).reshape(row_count, head_count, HEAD)
    front_half = per_head[..., :half_head]
    back_half = per_head[..., half_head:]
    turned = jnp.concatenate([front_half * cosine + back_half * sine_part, back_half * cosine - front_half * sine_part], axis=-1)
    return turned.reshape(row_count, head_count * HEAD).astype(jnp.bfloat16)

def doc_positions(sequence_ids):
    token_index = jnp.arange(sequence_ids.shape[0], dtype=jnp.int32)
    starts = jnp.where(sequence_ids == begin_token, token_index, -1)
    return token_index - lax.cummax(starts, axis=0)

def reference(token_ids, inputs, key_cotangent, key_weight, adam_m, adam_v, frag_local, frag_global, outer_mom, owner, fragment):
    replica_ids = token_ids.reshape(REPLICAS, SEQ)
    positions = jax.vmap(doc_positions)(replica_ids).reshape(REPLICAS * SEQ)
    key_grad = unrotate(key_cotangent, positions).reshape(REPLICAS, SEQ, -1)
    weight_bf = key_weight.astype(jnp.bfloat16)
    stacked = inputs.reshape(REPLICAS, SEQ, D)

    def one_replica(operands):
        rows_in, grads_in, weight_in = operands
        back_grad = lax.dot_general(grads_in, weight_in, (((1,), (1,)), ((), ())), preferred_element_type=jnp.float32).astype(jnp.bfloat16)
        input_blocks = rows_in.reshape(N_FSDP, TOK_DEV, D)
        grad_blocks = grads_in.reshape(N_FSDP, TOK_DEV, grads_in.shape[1])

        def add_block(running, block_pair):
            partial_value = lax.dot_general(block_pair[0], block_pair[1], (((0,), (0,)), ((), ())), preferred_element_type=jnp.float32)
            rounded = lax.optimization_barrier(partial_value.astype(jnp.bfloat16))
            return (running + rounded.astype(jnp.float32), None)
        summed = lax.scan(add_block, jnp.zeros((D, grads_in.shape[1]), jnp.float32), (input_blocks, grad_blocks))[0]
        return (back_grad, summed / SEQ)
    input_cotangent, weight_grad = lax.map(one_replica, (stacked, key_grad, weight_bf))
    moment_mean = beta_one * adam_m + (1.0 - beta_one) * weight_grad
    moment_square = beta_two * adam_v + (1.0 - beta_two) * weight_grad * weight_grad
    mean_hat = moment_mean / (1.0 - beta_one ** adam_step)
    square_hat = moment_square / (1.0 - beta_two ** adam_step)
    new_weight = key_weight - adam_lr * (mean_hat / (jnp.sqrt(square_hat) + adam_eps) + weight_decay * key_weight)
    slot_index = fragment.astype(jnp.int32)[:, None, None, None]
    local_slot = jnp.take_along_axis(frag_local, slot_index, axis=1)[:, 0]
    owner_rows = jnp.repeat(owner.astype(jnp.int32), D // N_FSDP)
    slot_rank = jnp.arange(REPLICAS, dtype=jnp.int32)[:, None]
    owned = (slot_rank == owner_rows[None, :])[:, :, None]
    state_global = lax.optimization_barrier(jnp.sum(jnp.where(owned, frag_global, 0.0), axis=0))
    state_mom = lax.optimization_barrier(jnp.sum(jnp.where(owned, outer_mom, 0.0), axis=0))
    outer_grad = state_global - lax.optimization_barrier(jnp.sum(local_slot, axis=0)) / REPLICAS
    mom_next = outer_momentum * state_mom + outer_grad
    synced_one = state_global - outer_lr * (outer_grad + outer_momentum * mom_next)
    synced = jnp.broadcast_to(synced_one[None], (REPLICAS, D, FW))
    new_outer_mom = jnp.where(owned, mom_next[None], outer_mom)
    return (input_cotangent.reshape(REPLICAS * SEQ, D), new_weight, moment_mean, moment_square, synced, new_outer_mom)
```

```python
import jax
import jax.numpy as jnp
from jax import lax
from jax.experimental import pallas as pl
from jax.experimental.pallas import tpu as pltpu
from jax.sharding import PartitionSpec as P

HEAD = 128
N_X, N_Z, N_CORE = 2, 8, 2

begin_token = 128000
rope_base = 500000.0
beta_one = 0.9
beta_two = 0.95
adam_lr = 0.001
adam_eps = 1e-08
adam_step = 10.0
weight_decay = 0.1
outer_lr = 0.7
outer_momentum = 0.9

PLACES = [(x, z, c) for x in range(N_X) for z in range(N_Z) for c in range(N_CORE)]
PEERS = [(0, 0), (0, 1), (1, 0), (1, 1)]


def place(x, z, c):
    return (x * N_Z + z % N_Z) * N_CORE + c


def along_z(value, distance):
    pairs = [(place(x, z, c), place(x, z + distance, c)) for x, z, c in PLACES]
    return lax.ppermute(value, "fsdp", pairs)


def with_peer(value, peer):
    flip_x, flip_c = PEERS[peer]
    pairs = [(place(x, z, c), place(x ^ flip_x, z, c ^ flip_c)) for x, z, c in PLACES]
    return lax.ppermute(value, "fsdp", pairs)


def unrotate_angles(positions):
    half_head = HEAD // 2
    frequency = jnp.float32(rope_base) ** (
        -(jnp.arange(half_head, dtype=jnp.float32) * (2.0 / HEAD))
    )
    return positions.astype(jnp.float32)[:, None] * frequency[None, :]


def place_index(x, z, c, peer):
    flip_x, flip_c = PEERS[peer]
    return ((x ^ flip_x) * N_Z + z) * N_CORE + (c ^ flip_c)


def peer_positions(token_ids, x, z, c):
    rows = token_ids.shape[0]
    ids = jnp.stack([token_ids] + [with_peer(token_ids, p) for p in (1, 2, 3)])
    indices = jnp.stack([place_index(x, z, c, p) for p in range(4)])
    token_index = indices[:, None] * rows + jnp.arange(rows, dtype=jnp.int32)[None, :]
    starts = jnp.where(ids == begin_token, token_index, -1)
    rank = jnp.arange(N_Z, dtype=jnp.int32)
    newest = jnp.where((rank == z)[:, None], jnp.max(starts, axis=1)[None, :], -1)
    for distance in (1, 2, 4):
        newest = jnp.maximum(newest, along_z(newest, distance))
    all_indices = jnp.stack([place_index(x, rank, c, p) for p in range(4)], axis=1)
    before = all_indices[None, :, :] < indices[:, None, None]
    earlier = jnp.max(jnp.where(before, newest[None], -1), axis=(1, 2))
    lane = jnp.arange(rows, dtype=jnp.int32)
    upto = lane[None, :] <= lane[:, None]
    latest = jnp.max(jnp.where(upto[None], starts[:, None, :], -1), axis=2)
    return token_index - jnp.maximum(latest, earlier[:, None])


def unrotate(cotangent, positions):
    row_count = cotangent.shape[0]
    head_count = cotangent.shape[1] // HEAD
    half_head = HEAD // 2
    angles = unrotate_angles(positions)
    cosine = jnp.cos(angles)[:, None, :]
    sine_part = jnp.sin(angles)[:, None, :]
    per_head = cotangent.astype(jnp.float32).reshape(row_count, head_count, HEAD)
    front_half = per_head[..., :half_head]
    back_half = per_head[..., half_head:]
    turned = jnp.concatenate(
        [front_half * cosine + back_half * sine_part, back_half * cosine - front_half * sine_part],
        axis=-1,
    )
    return turned.reshape(row_count, head_count * HEAD).astype(jnp.bfloat16)


NEAR = (0, 1, -1, 2, -2)
FAR = (3, -3, 4)


def column_of(base_ref, peer, ahead, width):
    step = lax.rem(base_ref[4] + (ahead + N_Z), N_Z)
    return pl.multiple_of(base_ref[peer] + step * (N_CORE * width), width)


def pack_columns(inputs, bases, width):
    tokens = inputs.shape[0]

    def kernel(base_ref, in_ref, *refs):
        outs, sem = refs[:8], refs[8]
        copies = []
        for part, steps in enumerate((NEAR, FAR)):
            for peer in range(4):
                for at, ahead in enumerate(steps):
                    copies.append(
                        pltpu.make_async_copy(
                            in_ref.at[:, pl.ds(column_of(base_ref, peer, ahead, width), width)],
                            outs[part * 4 + peer].at[:, pl.ds(at * width, width)],
                            sem.at[len(copies)],
                        )
                    )
        for copy in copies:
            copy.start()
        for copy in copies:
            copy.wait()

    shapes = [(tokens, len(steps) * width) for steps in (NEAR, FAR) for _ in range(4)]
    packed = pl.pallas_call(
        kernel,
        out_shape=[jax.ShapeDtypeStruct(shape, inputs.dtype) for shape in shapes],
        in_specs=[pl.BlockSpec(memory_space=pltpu.SMEM), pl.BlockSpec(memory_space=pl.ANY)],
        out_specs=[pl.BlockSpec(memory_space=pltpu.VMEM)] * 8,
        scratch_shapes=[pltpu.SemaphoreType.DMA((4 * N_Z,))],
        cost_estimate=pl.CostEstimate(flops=0, bytes_accessed=4 * inputs.size, transcendentals=0),
    )(bases, inputs)
    return packed[:4], packed[4:]


def unpack_columns(near, far, bases, width):
    tokens = near[0].shape[0]
    columns = 4 * N_Z * width

    def kernel(base_ref, *refs):
        ins, out_ref, sem = refs[:8], refs[8], refs[9]
        copies = []
        for part, steps in enumerate((NEAR, FAR)):
            for peer in range(4):
                for at, ahead in enumerate(steps):
                    copies.append(
                        pltpu.make_async_copy(
                            ins[part * 4 + peer].at[:, pl.ds(at * width, width)],
                            out_ref.at[:, pl.ds(column_of(base_ref, peer, ahead, width), width)],
                            sem.at[len(copies)],
                        )
                    )
        for copy in copies:
            copy.start()
        for copy in copies:
            copy.wait()

    return pl.pallas_call(
        kernel,
        out_shape=jax.ShapeDtypeStruct((tokens, columns), near[0].dtype),
        in_specs=[pl.BlockSpec(memory_space=pltpu.SMEM)] + [pl.BlockSpec(memory_space=pltpu.VMEM)] * 8,
        out_specs=pl.BlockSpec(memory_space=pl.ANY),
        scratch_shapes=[pltpu.SemaphoreType.DMA((4 * N_Z,))],
        cost_estimate=pl.CostEstimate(flops=0, bytes_accessed=4 * tokens * columns, transcendentals=0),
    )(bases, *near, *far)


def back_products(grads, weights):
    tokens, depth = grads.shape[1:]
    rows = weights[0].shape[0]
    count = len(weights)

    def kernel(g_ref, *refs):
        w_refs, outs = refs[:count], refs[count:]
        grad = g_ref[...].reshape(4 * tokens, depth)
        for at, w_ref in enumerate(w_refs):
            product = lax.dot_general(
                grad, w_ref[...], (((1,), (1,)), ((), ())), preferred_element_type=jnp.float32
            ).astype(jnp.bfloat16)
            for peer in range(4):
                outs[peer][:, at * rows : (at + 1) * rows] = product[peer * tokens : (peer + 1) * tokens]

    return pl.pallas_call(
        kernel,
        out_shape=[jax.ShapeDtypeStruct((tokens, count * rows), jnp.bfloat16)] * 4,
        in_specs=[pl.BlockSpec(memory_space=pltpu.VMEM)] * (1 + count),
        out_specs=[pl.BlockSpec(memory_space=pltpu.VMEM)] * 4,
        cost_estimate=pl.CostEstimate(
            flops=8 * tokens * depth * count * rows,
            bytes_accessed=2 * (4 * tokens * depth + count * rows * depth + 4 * tokens * count * rows),
            transcendentals=0,
        ),
    )(grads, *weights)


def weight_products(rows_in, grads, blocks):
    tokens, depth = grads.shape[1:]
    rows = rows_in[0].shape[1] // blocks

    def kernel(g_ref, *refs):
        ins, outs = refs[:4], refs[4:]
        for at, out in enumerate(outs):
            total = None
            for peer in range(4):
                term = lax.dot_general(
                    ins[peer][:, at * rows : (at + 1) * rows],
                    g_ref[peer],
                    (((0,), (0,)), ((), ())),
                    preferred_element_type=jnp.float32,
                )
                total = term if total is None else total + term
            out[...] = total.astype(jnp.bfloat16)

    return pl.pallas_call(
        kernel,
        out_shape=[jax.ShapeDtypeStruct((rows, depth), jnp.bfloat16)] * blocks,
        in_specs=[pl.BlockSpec(memory_space=pltpu.VMEM)] * 5,
        out_specs=[pl.BlockSpec(memory_space=pltpu.VMEM)] * blocks,
        cost_estimate=pl.CostEstimate(
            flops=8 * tokens * depth * blocks * rows,
            bytes_accessed=2 * (4 * tokens * depth + blocks * rows * depth + 4 * tokens * blocks * rows),
            transcendentals=0,
        ),
    )(grads, *rows_in)


def adam(forward, backward, own, key_weight, adam_m, adam_v, seq_len):
    rows, columns = own.shape
    step_rows = rows // 4

    def kernel(f_ref, b_ref, o_ref, w_ref, m_ref, v_ref, nw_ref, nm_ref, nv_ref):
        total = (
            f_ref[...].astype(jnp.float32)
            + b_ref[...].astype(jnp.float32)
            + o_ref[...].astype(jnp.float32)
        )
        grad = total / seq_len
        weight = w_ref[0]
        mean = beta_one * m_ref[0] + (1.0 - beta_one) * grad
        square = beta_two * v_ref[0] + (1.0 - beta_two) * grad * grad
        mean_hat = mean / (1.0 - beta_one**adam_step)
        square_hat = square / (1.0 - beta_two**adam_step)
        nm_ref[0] = mean
        nv_ref[0] = square
        nw_ref[0] = weight - adam_lr * (
            mean_hat / (jnp.sqrt(square_hat) + adam_eps) + weight_decay * weight
        )

    flat = pl.BlockSpec((step_rows, columns), lambda i: (i, 0))
    deep = pl.BlockSpec((1, step_rows, columns), lambda i: (0, i, 0))
    return pl.pallas_call(
        kernel,
        grid=(4,),
        out_shape=[jax.ShapeDtypeStruct((1, rows, columns), jnp.float32)] * 3,
        in_specs=[flat] * 3 + [deep] * 3,
        out_specs=[deep] * 3,
        cost_estimate=pl.CostEstimate(flops=20 * own.size, bytes_accessed=30 * own.size, transcendentals=own.size),
    )(forward, backward, own, key_weight, adam_m, adam_v)


def ring_gather(block):
    half = block.shape[0] // 2
    held = {0: block}
    behind = ahead = block
    for step in (1, 2, 3):
        behind, ahead = along_z(behind, 1), along_z(ahead, -1)
        held[-step], held[step] = behind, ahead
    held[4] = jnp.concatenate([along_z(behind[:half], 1), along_z(ahead[half:], -1)])
    return held


def added(arrived, term):
    return (arrived.astype(jnp.float32) + term.astype(jnp.float32)).astype(jnp.bfloat16)


def ring_reduce_far(blocks):
    half = blocks[4].shape[0] // 2
    forward = along_z(blocks[4][:half], 1)
    backward = along_z(blocks[4][half:], -1)
    term = blocks[3]
    forward = along_z(jnp.concatenate([added(forward, term[:half]), term[half:]]), 1)
    term = blocks[-3]
    backward = along_z(jnp.concatenate([term[:half], added(backward, term[half:])]), -1)
    return forward, backward


def ring_reduce_near(forward, backward, blocks):
    for ahead in (2, 1):
        forward = along_z(added(forward, blocks[ahead]), 1)
        backward = along_z(added(backward, blocks[-ahead]), -1)
    return forward, backward, blocks[0]


def outer_sync(frag_local, frag_global, outer_mom, owner, fragment):
    replica_count = lax.axis_size("replica")
    is_owner = lax.axis_index("replica") == owner[0]
    gain = outer_lr * (1.0 + outer_momentum)
    mom_gain = outer_lr * outer_momentum * outer_momentum
    local_slot = lax.dynamic_index_in_dim(frag_local[0], fragment[0], 0, keepdims=False)
    state_global, state_mom = frag_global[0], outer_mom[0]
    synced = (gain / replica_count) * local_slot + jnp.where(
        is_owner, (1.0 - gain) * state_global - mom_gain * state_mom, 0.0
    )
    for flip in (1, 2, 4):
        pairs = [(r, r ^ flip) for r in range(replica_count)]
        arrived = lax.ppermute(synced.astype(jnp.bfloat16), "replica", pairs)
        synced = synced + arrived.astype(jnp.float32)
    outer_grad = (state_global - mom_gain * state_mom - synced) / gain
    mom_next = outer_momentum * state_mom + outer_grad
    return synced[None], jnp.where(is_owner, mom_next, state_mom)[None]


def on_device(
    token_ids,
    inputs,
    key_cotangent,
    key_weight,
    adam_m,
    adam_v,
    frag_local,
    frag_global,
    outer_mom,
    owner,
    fragment,
):
    rows_here = inputs.shape[0]
    width = key_weight.shape[1]
    seq_len = rows_here * lax.axis_size("fsdp")
    index = lax.axis_index("fsdp")
    x, z, c = index // (N_Z * N_CORE), (index // N_CORE) % N_Z, index % N_CORE

    bases = jnp.stack(
        [((x ^ flip_x) * N_Z * N_CORE + (c ^ flip_c)) * width for flip_x, flip_c in PEERS] + [z]
    ).astype(jnp.int32)

    cotangents = jnp.concatenate([key_cotangent] + [with_peer(key_cotangent, p) for p in (1, 2, 3)])
    near, far = pack_columns(inputs, bases, width)
    far = [far[0]] + [with_peer(far[p], p) for p in (1, 2, 3)]
    near = [near[0]] + [with_peer(near[p], p) for p in (1, 2, 3)]
    positions = peer_positions(token_ids, x, z, c)
    weights = ring_gather(key_weight[0].astype(jnp.bfloat16))

    grads = unrotate(cotangents, positions.reshape(-1)).reshape(4, rows_here, -1)

    terms = dict(zip(FAR, weight_products(far, grads, len(FAR))))
    forward, backward = ring_reduce_far(terms)
    terms = dict(zip(NEAR, weight_products(near, grads, len(NEAR))))
    forward, backward, own = ring_reduce_near(forward, backward, terms)
    new_weight, new_m, new_v = adam(forward, backward, own, key_weight, adam_m, adam_v, seq_len)

    back = []
    for steps in (NEAR, FAR):
        part = back_products(grads, [weights[ahead] for ahead in steps])
        back.append([part[0]] + [with_peer(part[p], p) for p in (1, 2, 3)])
    input_cotangent = unpack_columns(*back, bases, width)

    synced, new_outer_mom = outer_sync(frag_local, frag_global, outer_mom, owner, fragment)
    return (input_cotangent, new_weight, new_m, new_v, synced, new_outer_mom)


def solution(mesh):
    in_specs = (
        P(("replica", "fsdp")),
        P(("replica", "fsdp"), None),
        P(("replica", "fsdp"), None),
        P("replica", "fsdp", None),
        P("replica", "fsdp", None),
        P("replica", "fsdp", None),
        P("replica", None, "fsdp", None),
        P("replica", "fsdp", None),
        P("replica", "fsdp", None),
        P("fsdp"),
        P("replica"),
    )
    out_specs = (
        P(("replica", "fsdp"), None),
        P("replica", "fsdp", None),
        P("replica", "fsdp", None),
        P("replica", "fsdp", None),
        P("replica", "fsdp", None),
        P("replica", "fsdp", None),
    )
    return jax.shard_map(
        on_device, mesh=mesh, in_specs=in_specs, out_specs=out_specs, check_vma=False
    )
```

```python
import jax
import jax.numpy as jnp
from jax import lax
from jax.experimental import pallas as pl
from jax.experimental.pallas import tpu as pltpu
from jax.sharding import PartitionSpec as P

HEAD = 128
N_X, N_Z, N_CORE = 2, 8, 2

begin_token = 128000
rope_base = 500000.0
beta_one = 0.9
beta_two = 0.95
adam_lr = 0.001
adam_eps = 1e-08
adam_step = 10.0
weight_decay = 0.1
outer_lr = 0.7
outer_momentum = 0.9

PLACES = [(x, z, c) for x in range(N_X) for z in range(N_Z) for c in range(N_CORE)]
PEERS = [(0, 0), (0, 1), (1, 0), (1, 1)]


def place(x, z, c):
    return (x * N_Z + z % N_Z) * N_CORE + c


def along_z(value, distance):
    pairs = [(place(x, z, c), place(x, z + distance, c)) for x, z, c in PLACES]
    return lax.ppermute(value, "fsdp", pairs)


def with_peer(value, peer):
    flip_x, flip_c = PEERS[peer]
    pairs = [(place(x, z, c), place(x ^ flip_x, z, c ^ flip_c)) for x, z, c in PLACES]
    return lax.ppermute(value, "fsdp", pairs)


def turn_tables(positions):
    half_head = HEAD // 2
    lane = jnp.arange(HEAD, dtype=jnp.int32)
    frequency = jnp.float32(rope_base) ** (
        -((lane % half_head).astype(jnp.float32) * (2.0 / HEAD))
    )
    angles = positions.astype(jnp.float32)[:, None] * frequency[None, :]
    sign = jnp.where(lane < half_head, 1.0, -1.0).astype(jnp.float32)
    return jnp.cos(angles), jnp.sin(angles) * sign[None, :]


def place_index(x, z, c, peer):
    flip_x, flip_c = PEERS[peer]
    return ((x ^ flip_x) * N_Z + z) * N_CORE + (c ^ flip_c)


def tie(value, *others):
    return lax.optimization_barrier((value, *others))[0]


FAR = (4, 3, -3)
NEAR = (2, -2, 1, -1, 0)
RING = (0, 1, -1, 2, -2, 3, -3, 4)


def room(mebibytes):
    return pltpu.CompilerParams(vmem_limit_bytes=mebibytes * 2**20)


def run_copies(copies):
    for copy in copies:
        copy.start()
    for copy in copies:
        copy.wait()


def vmem(count):
    return [pl.BlockSpec(memory_space=pltpu.VMEM)] * count


def pack_columns(inputs, cotangent, bases, width):
    tokens, depth = cotangent.shape
    steps = FAR + NEAR
    cut = len(FAR)

    def kernel(base_ref, in_ref, cot_ref, own, beside, far_2, far_3, near_2, near_3, sem):
        copies = []
        for peer in range(4):
            for at, ahead in enumerate(steps):
                step = lax.rem(base_ref[4] + (ahead + N_Z), N_Z)
                column = pl.multiple_of(base_ref[peer] + step * (N_CORE * width), width)
                if peer < 2:
                    out, first = (own, beside)[peer], at
                elif at < cut:
                    out, first = (far_2, far_3)[peer - 2], at
                else:
                    out, first = (near_2, near_3)[peer - 2], at - cut
                copies.append(
                    pltpu.make_async_copy(
                        in_ref.at[:, pl.ds(column, width)],
                        out.at[:, pl.ds(first * width, width)],
                        sem.at[len(copies)],
                    )
                )
        last = len(steps) * width
        copies.append(pltpu.make_async_copy(cot_ref, beside.at[:, pl.ds(last, depth)], sem.at[len(copies)]))
        run_copies(copies)

    widths = [len(steps) * width, len(steps) * width + depth]
    widths += [cut * width] * 2 + [len(NEAR) * width] * 2
    return pl.pallas_call(
        kernel,
        out_shape=[jax.ShapeDtypeStruct((tokens, columns), inputs.dtype) for columns in widths],
        in_specs=[pl.BlockSpec(memory_space=pltpu.SMEM)] + [pl.BlockSpec(memory_space=pl.ANY)] * 2,
        out_specs=vmem(6),
        scratch_shapes=[pltpu.SemaphoreType.DMA((4 * N_Z + 1,))],
        compiler_params=room(8),
        cost_estimate=pl.CostEstimate(flops=0, bytes_accessed=4 * inputs.size, transcendentals=0),
    )(bases, inputs, cotangent)


def unpack_columns(parts, bases, width):
    tokens = parts[0].shape[0]
    columns = 4 * N_Z * width

    def kernel(base_ref, *refs):
        ins, out_ref, sem = refs[:4], refs[4], refs[5]
        copies = []
        for peer in range(4):
            for at, ahead in enumerate(RING):
                step = lax.rem(base_ref[4] + (ahead + N_Z), N_Z)
                column = pl.multiple_of(base_ref[peer] + step * (N_CORE * width), width)
                copies.append(
                    pltpu.make_async_copy(
                        ins[peer].at[:, pl.ds(at * width, width)],
                        out_ref.at[:, pl.ds(column, width)],
                        sem.at[len(copies)],
                    )
                )
        run_copies(copies)

    return pl.pallas_call(
        kernel,
        out_shape=jax.ShapeDtypeStruct((tokens, columns), parts[0].dtype),
        in_specs=[pl.BlockSpec(memory_space=pltpu.SMEM)] + vmem(4),
        out_specs=pl.BlockSpec(memory_space=pl.ANY),
        scratch_shapes=[pltpu.SemaphoreType.DMA((4 * N_Z,))],
        compiler_params=room(8),
        cost_estimate=pl.CostEstimate(flops=0, bytes_accessed=4 * tokens * columns, transcendentals=0),
    )(bases, *parts)


def back_products(grads, weights):
    tokens, depth = grads.shape[0] // 4, grads.shape[1]
    rows = weights[0].shape[0]
    count = len(weights)

    def kernel(g_ref, *refs):
        w_refs, outs = refs[:count], refs[count:]
        grad = g_ref[...]
        for at, w_ref in enumerate(w_refs):
            product = lax.dot_general(
                grad, w_ref[...], (((1,), (1,)), ((), ())), preferred_element_type=jnp.float32
            ).astype(jnp.bfloat16)
            for peer in range(4):
                outs[peer][:, at * rows : (at + 1) * rows] = product[peer * tokens : (peer + 1) * tokens]

    return pl.pallas_call(
        kernel,
        out_shape=[jax.ShapeDtypeStruct((tokens, count * rows), jnp.bfloat16)] * 4,
        in_specs=vmem(1 + count),
        out_specs=vmem(4),
        compiler_params=room(16),
        cost_estimate=pl.CostEstimate(
            flops=8 * tokens * depth * count * rows,
            bytes_accessed=2 * (4 * tokens * depth + count * rows * depth + 4 * tokens * count * rows),
            transcendentals=0,
        ),
    )(grads, *weights)


def turn_and_multiply(cotangents, whole, far, tables, width):
    tokens, depth = cotangents[0].shape
    half = width // 2

    def kernel(c_ref, s_ref, cot, cot_2, cot_3, own, beside, far_2, far_3, turned, first, second):
        for peer, (ref, at_column) in enumerate(
            ((cot, 0), (beside, beside.shape[1] - depth), (cot_2, 0), (cot_3, 0))
        ):
            at = slice(peer * tokens, (peer + 1) * tokens)
            cosine, sine_part = c_ref[at, :], s_ref[at, :]
            for head in range(depth // HEAD):
                lane = at_column + head * HEAD
                value = ref[:, lane : lane + HEAD].astype(jnp.float32)
                other = pltpu.roll(value, HEAD // 2, 1)
                turned[at, head * HEAD : (head + 1) * HEAD] = (
                    value * cosine + other * sine_part
                ).astype(jnp.bfloat16)
        product = block_product((own, beside, far_2, far_3), 0, 0, width, turned[...])
        first[...] = product[:half]
        second[...] = product[half:]

    return pl.pallas_call(
        kernel,
        out_shape=[jax.ShapeDtypeStruct((4 * tokens, depth), jnp.bfloat16)]
        + [jax.ShapeDtypeStruct((half, depth), jnp.bfloat16)] * 2,
        in_specs=vmem(9),
        out_specs=vmem(3),
        compiler_params=room(12),
        cost_estimate=product_cost(tokens, depth, width, 1),
    )(*tables, *cotangents, *whole, *far)


def multiply(whole, part, grads, width, steps, part_steps):
    tokens, depth = grads.shape[0] // 4, grads.shape[1]
    order = FAR + NEAR

    def kernel(g_ref, *refs):
        ins, outs = refs[:4], refs[4:]
        grad = g_ref[...]
        for ahead, out in zip(steps, outs):
            out[...] = block_product(ins, order.index(ahead), part_steps.index(ahead), width, grad)

    return pl.pallas_call(
        kernel,
        out_shape=[jax.ShapeDtypeStruct((width, depth), jnp.bfloat16)] * len(steps),
        in_specs=vmem(5),
        out_specs=vmem(len(steps)),
        compiler_params=room(12),
        cost_estimate=product_cost(tokens, depth, width, len(steps)),
    )(grads, *whole, *part)


def block_product(ins, at_whole, at_part, width, grad):
    places = [at_whole * width] * 2 + [at_part * width] * 2
    block = jnp.concatenate([ref[:, p : p + width] for ref, p in zip(ins, places)], axis=0)
    return lax.dot_general(
        block, grad, (((0,), (0,)), ((), ())), preferred_element_type=jnp.float32
    ).astype(jnp.bfloat16)


def product_cost(tokens, depth, width, blocks):
    return pl.CostEstimate(
        flops=8 * tokens * depth * blocks * width,
        bytes_accessed=2 * (4 * tokens * depth + blocks * width * depth + 4 * tokens * blocks * width),
        transcendentals=0,
    )


def added(arrived, term):
    return (arrived.astype(jnp.float32) + term.astype(jnp.float32)).astype(jnp.bfloat16)


def add_halves(forward, backward, up, down):
    half = forward.shape[0]

    def kernel(f_ref, b_ref, u_ref, d_ref, f_out, b_out):
        f_out[:half] = added(f_ref[...], u_ref[:half])
        f_out[half:] = u_ref[half:]
        b_out[:half] = d_ref[:half]
        b_out[half:] = added(b_ref[...], d_ref[half:])

    return pl.pallas_call(
        kernel,
        out_shape=[jax.ShapeDtypeStruct(up.shape, up.dtype)] * 2,
        in_specs=vmem(4),
        out_specs=vmem(2),
        compiler_params=room(6),
        cost_estimate=pl.CostEstimate(flops=2 * up.size, bytes_accessed=10 * up.size, transcendentals=0),
    )(forward, backward, up, down)


def add_pair(forward, backward, up, down):
    def kernel(f_ref, b_ref, u_ref, d_ref, f_out, b_out):
        f_out[...] = added(f_ref[...], u_ref[...])
        b_out[...] = added(b_ref[...], d_ref[...])

    return pl.pallas_call(
        kernel,
        out_shape=[jax.ShapeDtypeStruct(up.shape, up.dtype)] * 2,
        in_specs=vmem(4),
        out_specs=vmem(2),
        compiler_params=room(6),
        cost_estimate=pl.CostEstimate(flops=2 * up.size, bytes_accessed=12 * up.size, transcendentals=0),
    )(forward, backward, up, down)


def adam(forward, backward, own, key_weight, adam_m, adam_v, seq_len):
    rows, columns = own.shape
    step_rows = rows // 4

    def kernel(f_ref, b_ref, o_ref, w_ref, m_ref, v_ref, nw_ref, nm_ref, nv_ref):
        total = (
            f_ref[...].astype(jnp.float32)
            + b_ref[...].astype(jnp.float32)
            + o_ref[...].astype(jnp.float32)
        )
        grad = total * (1.0 / seq_len)
        weight = w_ref[0]
        mean = beta_one * m_ref[0] + (1.0 - beta_one) * grad
        square = beta_two * v_ref[0] + (1.0 - beta_two) * grad * grad
        mean_hat = mean * (1.0 / (1.0 - beta_one**adam_step))
        square_hat = square * (1.0 / (1.0 - beta_two**adam_step))
        nm_ref[0] = mean
        nv_ref[0] = square
        nw_ref[0] = weight - adam_lr * (
            mean_hat / (jnp.sqrt(square_hat) + adam_eps) + weight_decay * weight
        )

    flat = pl.BlockSpec((step_rows, columns), lambda i: (i, 0))
    deep = pl.BlockSpec((1, step_rows, columns), lambda i: (0, i, 0))
    return pl.pallas_call(
        kernel,
        grid=(4,),
        out_shape=[jax.ShapeDtypeStruct((1, rows, columns), jnp.float32)] * 3,
        in_specs=[flat] * 3 + [deep] * 3,
        out_specs=[deep] * 3,
        compiler_params=room(12),
        cost_estimate=pl.CostEstimate(flops=20 * own.size, bytes_accessed=30 * own.size, transcendentals=own.size),
    )(forward, backward, own, key_weight, adam_m, adam_v)


def outer_sync(frag_local, frag_global, outer_mom, owner, fragment, after, before_swap):
    replica_count = lax.axis_size("replica")
    is_owner = tie(lax.axis_index("replica") == owner[0], after)
    gain = outer_lr * (1.0 + outer_momentum)
    mom_gain = outer_lr * outer_momentum * outer_momentum
    local_slot = lax.dynamic_index_in_dim(frag_local[0], fragment[0], 0, keepdims=False)
    state_global, state_mom = frag_global[0], outer_mom[0]
    synced = (gain / replica_count) * local_slot + jnp.where(
        is_owner, (1.0 - gain) * state_global - mom_gain * state_mom, 0.0
    )
    synced = tie(synced, before_swap)
    for flip in (1, 2, 4):
        pairs = [(r, r ^ flip) for r in range(replica_count)]
        arrived = lax.ppermute(synced.astype(jnp.bfloat16), "replica", pairs)
        synced = synced + arrived.astype(jnp.float32)
    outer_grad = (state_global - mom_gain * state_mom - synced) / gain
    mom_next = outer_momentum * state_mom + outer_grad
    return synced[None], jnp.where(is_owner, mom_next, state_mom)[None]


def on_device(
    token_ids,
    inputs,
    key_cotangent,
    key_weight,
    adam_m,
    adam_v,
    frag_local,
    frag_global,
    outer_mom,
    owner,
    fragment,
):
    rows_here = inputs.shape[0]
    width = key_weight.shape[1]
    seq_len = rows_here * lax.axis_size("fsdp")
    index = lax.axis_index("fsdp")
    x, z, c = index // (N_Z * N_CORE), (index // N_CORE) % N_Z, index % N_CORE

    bases = jnp.stack(
        [((x ^ flip_x) * N_Z * N_CORE + (c ^ flip_c)) * width for flip_x, flip_c in PEERS] + [z]
    ).astype(jnp.int32)

    ids = [token_ids] + [with_peer(token_ids, p) for p in (1, 2, 3)]
    across = with_peer(key_cotangent, 2)

    half = width // 2
    held = {0: tie(key_weight[0].astype(jnp.bfloat16), *ids[1:])}
    held[-1], held[1] = along_z(held[0], 1), along_z(held[0], -1)

    own, *packed = pack_columns(inputs, key_cotangent, tie(bases, *ids[1:]), width)
    far = [with_peer(packed[1], 2), with_peer(packed[2], 3)]
    whole = [own, with_peer(packed[0], 1)]
    cotangents = [key_cotangent, across, with_peer(tie(across, packed[0]), 1)]

    ids = jnp.stack(ids)
    indices = jnp.stack([place_index(x, z, c, p) for p in range(4)])
    token_index = indices[:, None] * rows_here + jnp.arange(rows_here, dtype=jnp.int32)[None, :]
    starts = jnp.where(ids == begin_token, token_index, -1)
    rank = jnp.arange(N_Z, dtype=jnp.int32)
    newest = jnp.where((rank == z)[:, None], jnp.max(starts, axis=1)[None, :], -1)
    newest = jnp.maximum(newest, jnp.maximum(along_z(newest, 1), along_z(newest, -1)))
    newest = tie(newest, packed[0], held[1], held[-1])
    newest = jnp.maximum(newest, jnp.maximum(along_z(newest, 3), along_z(newest, -3)))
    held[-2], held[2] = along_z(held[-1], 1), along_z(held[1], -1)
    all_indices = jnp.stack([place_index(x, rank, c, p) for p in range(4)], axis=1)
    before = all_indices[None, :, :] < indices[:, None, None]
    earlier = jnp.max(jnp.where(before, newest[None], -1), axis=(1, 2))
    lane = jnp.arange(rows_here, dtype=jnp.int32)
    upto = lane[None, :] <= lane[:, None]
    latest = jnp.max(jnp.where(upto[None], starts[:, None, :], -1), axis=2)
    positions = token_index - jnp.maximum(latest, earlier[:, None])
    tables = turn_tables(tie(positions, whole[1], far[0], far[1]).reshape(-1))

    near = [with_peer(tie(packed[3], newest), 2), with_peer(tie(packed[4], newest), 3)]

    grads, first, second = turn_and_multiply(cotangents, whole, far, tables, width)
    forward, backward = along_z(first, 1), along_z(second, -1)
    up, down = multiply(whole, far, grads, width, (3, -3), FAR)
    up = tie(up, held[2], held[-2])
    held[-3], held[3] = along_z(held[-2], 1), along_z(held[2], -1)
    summed = add_halves(forward, backward, up, down)
    forward, backward = along_z(summed[0], 1), along_z(summed[1], -1)
    up, down, up_1, down_1, term = multiply(whole, near, tie(grads, summed[0]), width, NEAR, NEAR)
    opposite = along_z(held[-3][:half], 1), along_z(held[3][half:], -1)
    forward, backward = add_pair(forward, backward, tie(up, held[3], held[-3]), down)
    forward, backward = along_z(forward, 1), along_z(backward, -1)

    synced, new_outer_mom = outer_sync(frag_local, frag_global, outer_mom, owner, fragment, newest, term)
    held[4] = jnp.concatenate(opposite)
    back = back_products(grads, [held[ahead] for ahead in RING])
    parts = [back[0]] + [with_peer(back[p], p) for p in (1, 2, 3)]

    forward, backward = add_pair(forward, backward, tie(up_1, back[0]), down_1)
    forward, backward = along_z(forward, 1), along_z(backward, -1)
    input_cotangent = unpack_columns(parts, bases, width)
    term = tie(term, input_cotangent)
    new_weight, new_m, new_v = adam(forward, backward, term, key_weight, adam_m, adam_v, seq_len)
    return (input_cotangent, new_weight, new_m, new_v, synced, new_outer_mom)


def solution(mesh):
    in_specs = (
        P(("replica", "fsdp")),
        P(("replica", "fsdp"), None),
        P(("replica", "fsdp"), None),
        P("replica", "fsdp", None),
        P("replica", "fsdp", None),
        P("replica", "fsdp", None),
        P("replica", None, "fsdp", None),
        P("replica", "fsdp", None),
        P("replica", "fsdp", None),
        P("fsdp"),
        P("replica"),
    )
    out_specs = (
        P(("replica", "fsdp"), None),
        P("replica", "fsdp", None),
        P("replica", "fsdp", None),
        P("replica", "fsdp", None),
        P("replica", "fsdp", None),
        P("replica", "fsdp", None),
    )
    return jax.shard_map(
        on_device, mesh=mesh, in_specs=in_specs, out_specs=out_specs, check_vma=False
    )
```

```python
import jax
import jax.numpy as jnp
from jax import lax
from jax.experimental import pallas as pl
from jax.experimental.pallas import tpu as pltpu
from jax.sharding import PartitionSpec as P

HEAD = 128
N_X, N_Z, N_CORE = 2, 8, 2

begin_token = 128000
rope_base = 500000.0
beta_one = 0.9
beta_two = 0.95
adam_lr = 0.001
adam_eps = 1e-08
adam_step = 10.0
weight_decay = 0.1
outer_lr = 0.7
outer_momentum = 0.9

PLACES = [(x, z, c) for x in range(N_X) for z in range(N_Z) for c in range(N_CORE)]
PEERS = [(0, 0), (0, 1), (1, 0), (1, 1)]


def place(x, z, c):
    return (x * N_Z + z % N_Z) * N_CORE + c


def along_z(value, distance):
    pairs = [(place(x, z, c), place(x, z + distance, c)) for x, z, c in PLACES]
    return lax.ppermute(value, "fsdp", pairs)


def with_peer(value, peer):
    flip_x, flip_c = PEERS[peer]
    pairs = [(place(x, z, c), place(x ^ flip_x, z, c ^ flip_c)) for x, z, c in PLACES]
    return lax.ppermute(value, "fsdp", pairs)


def turn_tables(positions):
    half_head = HEAD // 2
    lane = jnp.arange(HEAD, dtype=jnp.int32)
    frequency = jnp.float32(rope_base) ** (
        -((lane % half_head).astype(jnp.float32) * (2.0 / HEAD))
    )
    angles = positions.astype(jnp.float32)[:, None] * frequency[None, :]
    sign = jnp.where(lane < half_head, 1.0, -1.0).astype(jnp.float32)
    return jnp.cos(angles), jnp.sin(angles) * sign[None, :]


def place_index(x, z, c, peer):
    flip_x, flip_c = PEERS[peer]
    return ((x ^ flip_x) * N_Z + z) * N_CORE + (c ^ flip_c)


def tie(value, *others):
    return lax.optimization_barrier((value, *others))[0]


FAR = (4, 3, -3)
NEAR = (2, -2, 1, -1, 0)
RING = (0, 1, -1, 2, -2, 3, -3, 4)


def room(mebibytes):
    return pltpu.CompilerParams(vmem_limit_bytes=mebibytes * 2**20)


def run_copies(copies):
    for copy in copies:
        copy.start()
    for copy in copies:
        copy.wait()


def vmem(count):
    return [pl.BlockSpec(memory_space=pltpu.VMEM)] * count


def pack_columns(inputs, cotangent, bases, width):
    tokens, depth = cotangent.shape
    steps = FAR + NEAR
    cut = len(FAR)

    def kernel(base_ref, in_ref, cot_ref, own, beside, far_2, far_3, near_2, near_3, sem):
        copies = []
        for peer in range(4):
            for at, ahead in enumerate(steps):
                step = lax.rem(base_ref[4] + (ahead + N_Z), N_Z)
                column = pl.multiple_of(base_ref[peer] + step * (N_CORE * width), width)
                if peer < 2:
                    out, first = (own, beside)[peer], at
                elif at < cut:
                    out, first = (far_2, far_3)[peer - 2], at
                else:
                    out, first = (near_2, near_3)[peer - 2], at - cut
                copies.append(
                    pltpu.make_async_copy(
                        in_ref.at[:, pl.ds(column, width)],
                        out.at[:, pl.ds(first * width, width)],
                        sem.at[len(copies)],
                    )
                )
        last = len(steps) * width
        copies.append(pltpu.make_async_copy(cot_ref, beside.at[:, pl.ds(last, depth)], sem.at[len(copies)]))
        run_copies(copies)

    widths = [len(steps) * width, len(steps) * width + depth]
    widths += [cut * width] * 2 + [len(NEAR) * width] * 2
    return pl.pallas_call(
        kernel,
        out_shape=[jax.ShapeDtypeStruct((tokens, columns), inputs.dtype) for columns in widths],
        in_specs=[pl.BlockSpec(memory_space=pltpu.SMEM)] + [pl.BlockSpec(memory_space=pl.ANY)] * 2,
        out_specs=vmem(6),
        scratch_shapes=[pltpu.SemaphoreType.DMA((4 * N_Z + 1,))],
        compiler_params=room(8),
        cost_estimate=pl.CostEstimate(flops=0, bytes_accessed=4 * inputs.size, transcendentals=0),
    )(bases, inputs, cotangent)


def unpack_columns(parts, bases, width):
    tokens = parts[0].shape[0]
    columns = 4 * N_Z * width

    def kernel(base_ref, *refs):
        ins, out_ref, sem = refs[:4], refs[4], refs[5]
        copies = []
        for peer in range(4):
            for at, ahead in enumerate(RING):
                step = lax.rem(base_ref[4] + (ahead + N_Z), N_Z)
                column = pl.multiple_of(base_ref[peer] + step * (N_CORE * width), width)
                copies.append(
                    pltpu.make_async_copy(
                        ins[peer].at[:, pl.ds(at * width, width)],
                        out_ref.at[:, pl.ds(column, width)],
                        sem.at[len(copies)],
                    )
                )
        run_copies(copies)

    return pl.pallas_call(
        kernel,
        out_shape=jax.ShapeDtypeStruct((tokens, columns), parts[0].dtype),
        in_specs=[pl.BlockSpec(memory_space=pltpu.SMEM)] + vmem(4),
        out_specs=pl.BlockSpec(memory_space=pl.ANY),
        scratch_shapes=[pltpu.SemaphoreType.DMA((4 * N_Z,))],
        compiler_params=room(8),
        cost_estimate=pl.CostEstimate(flops=0, bytes_accessed=4 * tokens * columns, transcendentals=0),
    )(bases, *parts)


def back_products(grads, weights):
    tokens, depth = grads.shape[0] // 4, grads.shape[1]
    rows = weights[0].shape[0]
    count = len(weights)

    def kernel(g_ref, *refs):
        w_refs, outs = refs[:count], refs[count:]
        grad = g_ref[...]
        for at, w_ref in enumerate(w_refs):
            product = lax.dot_general(
                grad, w_ref[...], (((1,), (1,)), ((), ())), preferred_element_type=jnp.float32
            ).astype(jnp.bfloat16)
            for peer in range(4):
                outs[peer][:, at * rows : (at + 1) * rows] = product[peer * tokens : (peer + 1) * tokens]

    return pl.pallas_call(
        kernel,
        out_shape=[jax.ShapeDtypeStruct((tokens, count * rows), jnp.bfloat16)] * 4,
        in_specs=vmem(1 + count),
        out_specs=vmem(4),
        compiler_params=room(16),
        cost_estimate=pl.CostEstimate(
            flops=8 * tokens * depth * count * rows,
            bytes_accessed=2 * (4 * tokens * depth + count * rows * depth + 4 * tokens * count * rows),
            transcendentals=0,
        ),
    )(grads, *weights)


def turn_and_multiply(cotangents, whole, far, tables, width):
    tokens, depth = cotangents[0].shape
    half = width // 2

    def kernel(c_ref, s_ref, cot, cot_2, cot_3, own, beside, far_2, far_3, turned, first, second):
        for peer, (ref, at_column) in enumerate(
            ((cot, 0), (beside, beside.shape[1] - depth), (cot_2, 0), (cot_3, 0))
        ):
            at = slice(peer * tokens, (peer + 1) * tokens)
            cosine, sine_part = c_ref[at, :], s_ref[at, :]
            for head in range(depth // HEAD):
                lane = at_column + head * HEAD
                value = ref[:, lane : lane + HEAD].astype(jnp.float32)
                other = pltpu.roll(value, HEAD // 2, 1)
                turned[at, head * HEAD : (head + 1) * HEAD] = (
                    value * cosine + other * sine_part
                ).astype(jnp.bfloat16)
        product = block_product((own, beside, far_2, far_3), 0, 0, width, turned[...])
        first[...] = product[:half]
        second[...] = product[half:]

    return pl.pallas_call(
        kernel,
        out_shape=[jax.ShapeDtypeStruct((4 * tokens, depth), jnp.bfloat16)]
        + [jax.ShapeDtypeStruct((half, depth), jnp.bfloat16)] * 2,
        in_specs=vmem(9),
        out_specs=vmem(3),
        compiler_params=room(12),
        cost_estimate=product_cost(tokens, depth, width, 1),
    )(*tables, *cotangents, *whole, *far)


def multiply(whole, part, grads, width, steps, part_steps):
    tokens, depth = grads.shape[0] // 4, grads.shape[1]
    order = FAR + NEAR

    def kernel(g_ref, *refs):
        ins, outs = refs[:4], refs[4:]
        grad = g_ref[...]
        for ahead, out in zip(steps, outs):
            out[...] = block_product(ins, order.index(ahead), part_steps.index(ahead), width, grad)

    return pl.pallas_call(
        kernel,
        out_shape=[jax.ShapeDtypeStruct((width, depth), jnp.bfloat16)] * len(steps),
        in_specs=vmem(5),
        out_specs=vmem(len(steps)),
        compiler_params=room(12),
        cost_estimate=product_cost(tokens, depth, width, len(steps)),
    )(grads, *whole, *part)


def block_product(ins, at_whole, at_part, width, grad):
    places = [at_whole * width] * 2 + [at_part * width] * 2
    block = jnp.concatenate([ref[:, p : p + width] for ref, p in zip(ins, places)], axis=0)
    return lax.dot_general(
        block, grad, (((0,), (0,)), ((), ())), preferred_element_type=jnp.float32
    ).astype(jnp.bfloat16)


def product_cost(tokens, depth, width, blocks):
    return pl.CostEstimate(
        flops=8 * tokens * depth * blocks * width,
        bytes_accessed=2 * (4 * tokens * depth + blocks * width * depth + 4 * tokens * blocks * width),
        transcendentals=0,
    )


def added(arrived, term):
    return (arrived.astype(jnp.float32) + term.astype(jnp.float32)).astype(jnp.bfloat16)


def add_halves(forward, backward, up, down):
    half = forward.shape[0]

    def kernel(f_ref, b_ref, u_ref, d_ref, f_out, b_out):
        f_out[:half] = added(f_ref[...], u_ref[:half])
        f_out[half:] = u_ref[half:]
        b_out[:half] = d_ref[:half]
        b_out[half:] = added(b_ref[...], d_ref[half:])

    return pl.pallas_call(
        kernel,
        out_shape=[jax.ShapeDtypeStruct(up.shape, up.dtype)] * 2,
        in_specs=vmem(4),
        out_specs=vmem(2),
        compiler_params=room(6),
        cost_estimate=pl.CostEstimate(flops=2 * up.size, bytes_accessed=10 * up.size, transcendentals=0),
    )(forward, backward, up, down)


def add_pair(forward, backward, up, down):
    def kernel(f_ref, b_ref, u_ref, d_ref, f_out, b_out):
        f_out[...] = added(f_ref[...], u_ref[...])
        b_out[...] = added(b_ref[...], d_ref[...])

    return pl.pallas_call(
        kernel,
        out_shape=[jax.ShapeDtypeStruct(up.shape, up.dtype)] * 2,
        in_specs=vmem(4),
        out_specs=vmem(2),
        compiler_params=room(6),
        cost_estimate=pl.CostEstimate(flops=2 * up.size, bytes_accessed=12 * up.size, transcendentals=0),
    )(forward, backward, up, down)


def adam(forward, backward, own, key_weight, adam_m, adam_v, seq_len):
    rows, columns = own.shape
    step_rows = rows // 4

    def kernel(f_ref, b_ref, o_ref, w_ref, m_ref, v_ref, nw_ref, nm_ref, nv_ref):
        total = (
            f_ref[...].astype(jnp.float32)
            + b_ref[...].astype(jnp.float32)
            + o_ref[...].astype(jnp.float32)
        )
        grad = total * (1.0 / seq_len)
        weight = w_ref[0]
        mean = beta_one * m_ref[0] + (1.0 - beta_one) * grad
        square = beta_two * v_ref[0] + (1.0 - beta_two) * grad * grad
        mean_hat = mean * (1.0 / (1.0 - beta_one**adam_step))
        square_hat = square * (1.0 / (1.0 - beta_two**adam_step))
        nm_ref[0] = mean
        nv_ref[0] = square
        nw_ref[0] = weight - adam_lr * (
            mean_hat / (jnp.sqrt(square_hat) + adam_eps) + weight_decay * weight
        )

    flat = pl.BlockSpec((step_rows, columns), lambda i: (i, 0))
    deep = pl.BlockSpec((1, step_rows, columns), lambda i: (0, i, 0))
    return pl.pallas_call(
        kernel,
        grid=(4,),
        out_shape=[jax.ShapeDtypeStruct((1, rows, columns), jnp.float32)] * 3,
        in_specs=[flat] * 3 + [deep] * 3,
        out_specs=[deep] * 3,
        compiler_params=room(12),
        cost_estimate=pl.CostEstimate(flops=20 * own.size, bytes_accessed=30 * own.size, transcendentals=own.size),
    )(forward, backward, own, key_weight, adam_m, adam_v)


def outer_sync(frag_local, frag_global, outer_mom, owner, fragment, after, before_swap, before_last):
    replica_count = lax.axis_size("replica")
    is_owner = tie(lax.axis_index("replica") == owner[0], after)
    gain = outer_lr * (1.0 + outer_momentum)
    mom_gain = outer_lr * outer_momentum * outer_momentum
    local_slot = lax.dynamic_index_in_dim(frag_local[0], fragment[0], 0, keepdims=False)
    state_global, state_mom = frag_global[0], outer_mom[0]
    synced = (gain / replica_count) * local_slot + jnp.where(
        is_owner, (1.0 - gain) * state_global - mom_gain * state_mom, 0.0
    )
    synced = tie(synced, before_swap)
    for flip in (1, 2, 4):
        synced = tie(synced, before_last) if flip == 4 else synced
        pairs = [(r, r ^ flip) for r in range(replica_count)]
        arrived = lax.ppermute(synced.astype(jnp.bfloat16), "replica", pairs)
        synced = synced + arrived.astype(jnp.float32)
    outer_grad = (state_global - mom_gain * state_mom - synced) / gain
    mom_next = outer_momentum * state_mom + outer_grad
    return synced[None], jnp.where(is_owner, mom_next, state_mom)[None]


def on_device(
    token_ids,
    inputs,
    key_cotangent,
    key_weight,
    adam_m,
    adam_v,
    frag_local,
    frag_global,
    outer_mom,
    owner,
    fragment,
):
    rows_here = inputs.shape[0]
    width = key_weight.shape[1]
    seq_len = rows_here * lax.axis_size("fsdp")
    index = lax.axis_index("fsdp")
    x, z, c = index // (N_Z * N_CORE), (index // N_CORE) % N_Z, index % N_CORE

    bases = jnp.stack(
        [((x ^ flip_x) * N_Z * N_CORE + (c ^ flip_c)) * width for flip_x, flip_c in PEERS] + [z]
    ).astype(jnp.int32)

    ids = [token_ids] + [with_peer(token_ids, p) for p in (1, 2, 3)]
    across = with_peer(key_cotangent, 2)

    half = width // 2
    held = {0: key_weight[0].astype(jnp.bfloat16)}
    held[-1], held[1] = along_z(held[0], 1), along_z(held[0], -1)

    own, *packed = pack_columns(inputs, key_cotangent, tie(bases, *ids[1:]), width)
    far = [with_peer(packed[1], 2), with_peer(packed[2], 3)]
    whole = [own, with_peer(packed[0], 1)]
    cotangents = [key_cotangent, across, with_peer(tie(across, packed[0]), 1)]

    ids = jnp.stack(ids)
    indices = jnp.stack([place_index(x, z, c, p) for p in range(4)])
    token_index = indices[:, None] * rows_here + jnp.arange(rows_here, dtype=jnp.int32)[None, :]
    starts = jnp.where(ids == begin_token, token_index, -1)
    rank = jnp.arange(N_Z, dtype=jnp.int32)
    newest = jnp.where((rank == z)[:, None], jnp.max(starts, axis=1)[None, :], -1)
    newest = jnp.maximum(newest, jnp.maximum(along_z(newest, 1), along_z(newest, -1)))
    newest = tie(newest, packed[0], held[1], held[-1])
    newest = jnp.maximum(newest, jnp.maximum(along_z(newest, 3), along_z(newest, -3)))
    held[-2], held[2] = along_z(held[-1], 1), along_z(held[1], -1)
    all_indices = jnp.stack([place_index(x, rank, c, p) for p in range(4)], axis=1)
    before = all_indices[None, :, :] < indices[:, None, None]
    earlier = jnp.max(jnp.where(before, newest[None], -1), axis=(1, 2))
    lane = jnp.arange(rows_here, dtype=jnp.int32)
    upto = lane[None, :] <= lane[:, None]
    latest = jnp.max(jnp.where(upto[None], starts[:, None, :], -1), axis=2)
    positions = token_index - jnp.maximum(latest, earlier[:, None])
    tables = turn_tables(tie(positions, whole[1], far[0], far[1]).reshape(-1))

    near = [with_peer(tie(packed[3], newest), 2), with_peer(tie(packed[4], newest), 3)]

    grads, first, second = turn_and_multiply(cotangents, whole, far, tables, width)
    forward, backward = along_z(first, 1), along_z(second, -1)
    up, down = multiply(whole, far, grads, width, (3, -3), FAR)
    up = tie(up, held[2], held[-2])
    held[-3], held[3] = along_z(held[-2], 1), along_z(held[2], -1)
    summed = add_halves(forward, backward, up, down)
    forward, backward = along_z(summed[0], 1), along_z(summed[1], -1)
    up, down, up_1, down_1, term = multiply(whole, near, tie(grads, summed[0]), width, NEAR, NEAR)
    opposite = along_z(held[-3][:half], 1), along_z(held[3][half:], -1)
    forward, backward = add_pair(forward, backward, tie(up, held[3], held[-3]), down)
    forward, backward = along_z(forward, 1), along_z(backward, -1)

    held[4] = jnp.concatenate(opposite)
    back = back_products(grads, [held[ahead] for ahead in RING])
    synced, new_outer_mom = outer_sync(
        frag_local, frag_global, outer_mom, owner, fragment, newest, term, back[0]
    )
    parts = [back[0]] + [with_peer(back[p], p) for p in (1, 2, 3)]

    forward, backward = add_pair(forward, backward, tie(up_1, back[0]), down_1)
    forward, backward = along_z(forward, 1), along_z(backward, -1)
    input_cotangent = unpack_columns(parts, bases, width)
    term = tie(term, input_cotangent)
    new_weight, new_m, new_v = adam(forward, backward, term, key_weight, adam_m, adam_v, seq_len)
    return (input_cotangent, new_weight, new_m, new_v, synced, new_outer_mom)


def solution(mesh):
    in_specs = (
        P(("replica", "fsdp")),
        P(("replica", "fsdp"), None),
        P(("replica", "fsdp"), None),
        P("replica", "fsdp", None),
        P("replica", "fsdp", None),
        P("replica", "fsdp", None),
        P("replica", None, "fsdp", None),
        P("replica", "fsdp", None),
        P("replica", "fsdp", None),
        P("fsdp"),
        P("replica"),
    )
    out_specs = (
        P(("replica", "fsdp"), None),
        P("replica", "fsdp", None),
        P("replica", "fsdp", None),
        P("replica", "fsdp", None),
        P("replica", "fsdp", None),
        P("replica", "fsdp", None),
    )
    return jax.shard_map(
        on_device, mesh=mesh, in_specs=in_specs, out_specs=out_specs, check_vma=False
    )
```
